128 devices in a mesh: section: 8 (over y, core), dp: 16 (over x, z).
Axes of the slice: x: 4, y: 4, z: 4, core: 2. Of those that a mesh axis runs over, the one named last changes fastest.
Arguments:
- activations: bfloat16 [196608, 8192], P(('section', 'dp')), parts along dimension 0, may hold values from -36 to 36, as said below
- cotangent: bfloat16 [196608, 512], P(('section', 'dp')), parts along dimension 0, may hold values from -16 to 16, as said below
- weight: bfloat16 [65536, 512], P(('section', 'dp')), parts along dimension 0, may hold values from -0.0625 to 0.0625
- row_state: float32 [65536], P(('section', 'dp')), parts along dimension 0, may hold values from 81 to 7372800, as said below
- column_state: float32 [4096], P('section'), parts along dimension 0, may hold values from 307 to 835584, as said below
Outputs:
- new_weight: bfloat16 [65536, 512], P('section'), parts along dimension 0
- row_moment: float32 [65536], P(('section', 'dp')), parts along dimension 0
- column_moment: float32 [4096], P('section'), parts along dimension 0
The draws below stay inside these ranges and needn't reach their ends.
There are 8 independent parts, one for each index of `section`. The reference program is written for one: setup_inputs(seed, part) draws one part's arguments, and reference() takes and returns one part's arrays. A program takes and returns all parts, laid end to end along the dimension named above; each array names one. Nothing has to cross between parts.
Inputs may be any that keep to these rules, and one draw needn't show every extreme that they name: activations are finite. cotangent entries are finite. `row_state`: positive. `column_state`: positive.
All inputs are finite; a program needn't handle non-finite values.
Results may differ from the reference program's by a relative error of at most 0.017.
Values may be sent and summed in bfloat16 or wider, within the bound.
A program may use at most 128 MiB of HBM per device.

```python
import math
import jax
import jax.numpy as jnp
from jax import lax

D = 8192
FFS = 512
TOKENS = 24576
N_DP = 16


def input_scales(key):
    key = jax.random.fold_in(key, 11)
    sample = jax.random.uniform(key, (D,), jnp.float32, math.log(0.4), math.log(4.0))
    position = jnp.arange(D, dtype=jnp.float32) / D
    return jnp.exp(sample) * jnp.exp((position - 0.5) * math.log(3.0))


def output_scales(key):
    key = jax.random.fold_in(key, 12)
    sample = jax.random.uniform(key, (FFS,), jnp.float32, math.log(0.4), math.log(4.0))
    return jnp.exp(sample)


def entries(key, shape):
    sample = jnp.clip(jax.random.normal(key, shape, jnp.float32), -4.0, 4.0)
    return sample


def band_latent(key):
    key = jax.random.fold_in(key, 13)
    return entries(key, (TOKENS, 8))


def falling(first, last):
    position = jnp.arange(D, dtype=jnp.float32) / D
    return jnp.exp(math.log(first) + position * (math.log(last) - math.log(first)))


def draw_activations(key, part):
    scales = input_scales(key)
    latent = band_latent(key)
    key = jax.random.fold_in(key, 1)
    sample = entries(key, (TOKENS, D))
    shared = jnp.repeat(latent, D // 8, axis=1)
    mixed = (sample + 0.25 * shared) / math.sqrt(1.0625)
    return (mixed * scales[None, :]).astype(jnp.bfloat16)


def draw_cotangent(key, part):
    scales = output_scales(key)
    latent = band_latent(key)
    key = jax.random.fold_in(key, 2)
    noise_key = jax.random.fold_in(key, 21)
    order_key = jax.random.fold_in(key, 22)
    gain_key = jax.random.fold_in(key, 23)
    sample = entries(noise_key, (TOKENS, FFS))
    rank = jax.random.permutation(order_key, FFS)
    group = rank % 8
    linked = (rank < FFS // 2).astype(jnp.float32)
    boost = 1.0 + group.astype(jnp.float32) / 3.5
    gain = jnp.exp(jax.random.uniform(gain_key, (FFS,), jnp.float32, math.log(0.8), math.log(1.6)))
    strength = linked * gain * boost * math.sqrt(936.0 / max(TOKENS, 1024))
    coupled = jnp.take(latent, group, axis=1) * strength[None, :]
    total = jnp.clip(sample * scales[None, :] + coupled, -16.0, 16.0)
    return total.astype(jnp.bfloat16)


def draw_row_state(key, part):
    scales = input_scales(key)
    key = jax.random.fold_in(key, 3)
    factor = jnp.exp(jax.random.uniform(key, (D,), jnp.float32, math.log(0.5), math.log(2.0)))
    trend = falling(5.0, 0.02)
    return (TOKENS * 3.4396 * scales * scales * factor * trend).astype(jnp.float32)


def draw_column_state(key, part):
    scales = output_scales(key)
    key = jax.random.fold_in(key, 4)
    factor = jnp.exp(jax.random.uniform(key, (FFS,), jnp.float32, math.log(0.02), math.log(0.5)))
    return (TOKENS * 3.4396 * 1.2137 * scales * scales * factor).astype(jnp.float32)


def shard_levels(key, shape, shards, low, top_value):
    level = 1.0
    for dim, blocks in shards:
        steps = jax.random.uniform(jax.random.fold_in(jax.random.fold_in(key, 6), dim), (blocks,), jnp.float32, low / len(shards), top_value / len(shards))
        level = level * jnp.repeat(jnp.exp(steps), shape[dim] // blocks).reshape((-1,) + (1,) * (len(shape) - 1 - dim))
    return level


def gaussian(key, dims, scale, limit, cuts=(), held_as=jnp.bfloat16):
    array = scale * jax.random.normal(key, dims, jnp.float32)
    if cuts:
        array = array * shard_levels(key, dims, cuts, -0.22, 0.18)
    return jnp.clip(array, -limit, limit).astype(held_as)


def setup_inputs(seed: int = 0, part: int = 0) -> dict:
    seeds = jax.random.split(jax.random.key(seed), 6)
    own_keys = jax.random.split(jax.random.fold_in(seeds[5], part), 6)
    return {
        "activations": draw_activations(jax.random.fold_in(jax.random.fold_in(seeds[5], part), 71), part),
        "cotangent": draw_cotangent(jax.random.fold_in(jax.random.fold_in(seeds[5], part), 71), part),
        "weight": gaussian(own_keys[2], (D, FFS), D ** -0.5, 0.0625, ((0, 16),)),
        "row_state": draw_row_state(jax.random.fold_in(jax.random.fold_in(seeds[5], part), 71), part),
        "column_state": draw_column_state(jax.random.fold_in(jax.random.fold_in(seeds[5], part), 71), part),
    }


decay_rate = 0.8
learn_rate = 0.1
clip_level = 1.0
epsilon_one = 1e-30

def reference(activations, cotangent, weight, row_state, column_state):
    tok_blocks = activations.reshape(N_DP, TOKENS // N_DP, D)
    cot_blocks = cotangent.reshape(N_DP, TOKENS // N_DP, FFS)

    def accumulate(total, pair):
        left, right = pair
        term = jnp.dot(left.T, right, preferred_element_type=jnp.float32).astype(jnp.bfloat16)
        term = lax.optimization_barrier(term)
        return (total + term.astype(jnp.float32), None)
    start = jnp.zeros((D, FFS), jnp.float32)
    gradient, _ = lax.scan(accumulate, start, (tok_blocks, cot_blocks))
    squares = gradient * gradient + epsilon_one
    row_moment = decay_rate * row_state + (1.0 - decay_rate) * lax.optimization_barrier(jnp.mean(squares, axis=1))
    column_moment = decay_rate * column_state + (1.0 - decay_rate) * lax.optimization_barrier(jnp.mean(squares, axis=0))
    mean_row = jnp.mean(row_moment)
    update = gradient / jnp.sqrt(row_moment[:, None] * column_moment[None, :] / mean_row)
    ratio = jnp.sqrt(jnp.mean(update * update)) / clip_level
    fresh = weight.astype(jnp.float32) - learn_rate * update / jnp.maximum(1.0, ratio)
    return (fresh.astype(jnp.bfloat16), row_moment, column_moment)
```

```python
import functools

import jax
import jax.numpy as jnp
from jax import lax
from jax.experimental import pallas as pl
from jax.experimental.pallas import tpu as pltpu
from jax.sharding import PartitionSpec as P

MESH = pl.DeviceIdType.MESH
decay_rate = 0.8
learn_rate = 0.1
clip_level = 1.0
epsilon_one = 1e-30
SIDE = 4
FAR, NEXT, LAST, OWN = 0, 1, 2, 3
SLOTS = 3
F32 = jnp.float32
BF16 = jnp.bfloat16


def offset(k):
    return 2 - k + (k // 2) * (7 - 2 * k)


def kernel(
    act, cot, weight, row_state, col_state,
    out, row_out, col_out,
    abuf, cbuf, wbuf, grad, r1, r2, norm, fresh, msg, heard,
    a_sem, c_sem, w_sem, o_sem,
    s1, v1, s2, v2, ss, vs, g1s, g1v, f1s, f1v, g2s, g2v, f2s, f2v,
):
    me = lax.axis_index("dp")
    px, pz = me // SIDE, me % SIDE
    n = SIDE * SIDE
    q, ff = grad.shape[4], grad.shape[5]
    shard = 4 * q
    lanes = ff // 128

    def place(g, da, db):
        dx, dz = (da, db) if g == 0 else (db, da)
        return ((px + dx) % SIDE) * SIDE + (pz + dz) % SIDE

    def send(src, dst, ssem, rsem, target):
        return pltpu.make_async_remote_copy(
            src_ref=src, dst_ref=dst, send_sem=ssem, recv_sem=rsem,
            device_id={"dp": target}, device_id_type=MESH,
        )

    step = (1, SIDE - 1)

    def fetch(i, g):
        k, m = i // SIDE, i % SIDE
        col = place(g, offset(k), offset(m)) * shard + g * 2 * q
        return pltpu.make_async_copy(
            act.at[:, pl.ds(pl.multiple_of(col, 2 * q), 2 * q)],
            abuf.at[i % SLOTS, g], a_sem.at[i % SLOTS, g],
        )

    barrier = pltpu.get_barrier_semaphore()
    for j in range(1, n):
        pl.semaphore_signal(
            barrier, inc=1, device_id={"dp": (me + j) % n}, device_id_type=MESH
        )
    get_cot = pltpu.make_async_copy(cot, cbuf, c_sem)
    get_cot.start()
    for i in range(SLOTS - 1):
        for g in range(2):
            fetch(i, g).start()
    get_weight = pltpu.make_async_copy(weight, wbuf, w_sem)
    get_weight.start()
    get_cot.wait()

    def far1(g, d, m):
        return send(grad.at[g, FAR, m, d], r1.at[0, g, d, m],
                    s1.at[0, g, d, m], v1.at[0, g, d, m], place(g, step[d], 0))

    def near1(g, d, m):
        return send(grad.at[g, NEXT + d, m, 1 - d], r1.at[1, g, d, m],
                    s1.at[1, g, d, m], v1.at[1, g, d, m], place(g, step[d], 0))

    def both1(g, d, m):
        return send(grad.at[g, NEXT + d, m, d], r1.at[2, g, d, m],
                    s1.at[2, g, d, m], v1.at[2, g, d, m], place(g, step[d], 0))

    @pl.loop(0, SIDE * SIDE)
    def _(i):
        k, m = i // SIDE, i % SIDE
        for g in range(2):
            fetch(i, g).wait()

            @pl.when(i + SLOTS - 1 < SIDE * SIDE)
            def _():
                fetch(i + SLOTS - 1, g).start()

            part = lax.dot_general(
                abuf[i % SLOTS, g], cbuf[...], (((0,), (0,)), ((), ())),
                preferred_element_type=F32,
            ).astype(BF16)
            grad[g, k, m, 0] = part[:q]
            grad[g, k, m, 1] = part[q:]

        @pl.when(i == 0)
        def _():
            pl.semaphore_wait(barrier, n - 1)

        @pl.when(k == FAR)
        def _():
            for g in range(2):
                for d in range(2):
                    far1(g, d, m).start()

        @pl.when(k == NEXT)
        def _():
            for g in range(2):
                near1(g, 0, m).start()

        @pl.when(k == LAST)
        def _():
            for g in range(2):
                near1(g, 1, m).start()

    @pl.loop(0, SIDE)
    def _(m):
        for g in range(2):
            for d in range(2):
                far1(g, d, m).wait_recv()
                grad[g, NEXT + d, m, d] = (
                    grad[g, NEXT + d, m, d].astype(F32) + r1[0, g, d, m].astype(F32)
                ).astype(BF16)
                both1(g, d, m).start()

    def total1(g, m, h):
        both1(g, h, m).wait_recv()
        near1(g, 1 - h, m).wait_recv()
        return (
            grad[g, OWN, m, h].astype(F32) + r1[2, g, h, m].astype(F32)
        ) + r1[1, g, 1 - h, m].astype(F32)

    def far2(g, d):
        return send(grad.at[g, OWN, FAR, d], r2.at[0, g, d],
                    s2.at[0, g, d], v2.at[0, g, d], place(g, 0, step[d]))

    def near2(g, d):
        return send(grad.at[g, OWN, NEXT + d, 1 - d], r2.at[1, g, d],
                    s2.at[1, g, d], v2.at[1, g, d], place(g, 0, step[d]))

    def both2(g, d):
        return send(grad.at[g, OWN, NEXT + d, d], r2.at[2, g, d],
                    s2.at[2, g, d], v2.at[2, g, d], place(g, 0, step[d]))

    for g in range(2):
        for h in range(2):
            grad[g, OWN, FAR, h] = total1(g, FAR, h).astype(BF16)
            far2(g, h).start()
    for d in range(2):
        for g in range(2):
            for h in range(2):
                grad[g, OWN, NEXT + d, h] = total1(g, NEXT + d, h).astype(BF16)
            near2(g, d).start()
    for d in range(2):
        for g in range(2):
            far2(g, d).wait_recv()
            grad[g, OWN, NEXT + d, d] = (
                grad[g, OWN, NEXT + d, d].astype(F32) + r2[0, g, d].astype(F32)
            ).astype(BF16)
            both2(g, d).start()

    eye = lax.broadcasted_iota(jnp.int32, (q, q), 0) == lax.broadcasted_iota(jnp.int32, (q, q), 1)
    square_sum = jnp.zeros((1, ff), F32)
    update_sum = jnp.zeros((1, ff), F32)
    row_sum = jnp.zeros((1, 1), F32)
    for g in range(2):
        for h in range(2):
            i = 2 * g + h
            mine = total1(g, OWN, h)
            both2(g, h).wait_recv()
            near2(g, 1 - h).wait_recv()
            mine = (mine + r2[2, g, h].astype(F32)) + r2[1, g, 1 - h].astype(F32)
            squares = mine * mine + epsilon_one
            state = jnp.sum(jnp.where(eye, row_state[i:i + 1, :], 0.0), axis=1, keepdims=True)
            moment = decay_rate * state + (1.0 - decay_rate) * (
                jnp.sum(squares, axis=1, keepdims=True) / ff
            )
            row_out[i:i + 1, :] = jnp.sum(jnp.where(eye, moment, 0.0), axis=0, keepdims=True)
            scaled = mine * lax.rsqrt(moment)
            norm[i] = scaled
            square_sum += jnp.sum(squares, axis=0, keepdims=True)
            update_sum += jnp.sum(scaled * scaled, axis=0, keepdims=True)
            row_sum += jnp.sum(moment, axis=0, keepdims=True)
    msg[...] = jnp.zeros(msg.shape, F32)
    for j in range(lanes):
        msg[j:j + 1, :] = square_sum[:, 128 * j:128 * (j + 1)]
        msg[lanes + j:lanes + j + 1, :] = update_sum[:, 128 * j:128 * (j + 1)]
    msg[2 * lanes:2 * lanes + 1, :] = jnp.broadcast_to(row_sum, (1, 128))

    def tell(j):
        return send(msg, heard.at[me], ss.at[j], vs.at[me], (me + j) % n)

    def hear(j):
        other = (me + j) % n
        return send(msg, heard.at[other], ss.at[0], vs.at[other], other)

    for j in range(1, n):
        tell(j).start()
    heard[me] = msg[...]
    for j in range(1, n):
        hear(j).wait_recv()
    total = heard[0]
    for j in range(1, n):
        total = total + heard[j]
    col_moment = decay_rate * col_state[...] + (1.0 - decay_rate) * (total[:lanes] / (n * shard))
    col_out[...] = col_moment
    mean_row = jnp.max(total[2 * lanes:2 * lanes + 1], axis=1, keepdims=True) / (n * shard)
    update_mean = (
        jnp.sum(jnp.sum(total[lanes:2 * lanes] / col_moment, axis=1, keepdims=True), axis=0, keepdims=True)
        * mean_row / (n * shard * ff)
    )
    ratio = jnp.sqrt(update_mean) / clip_level
    factor = lax.rsqrt(col_moment) * (learn_rate * jnp.sqrt(mean_row) / jnp.maximum(1.0, ratio))

    def rows(dev, g, h):
        return out.at[pl.ds(pl.multiple_of(dev * shard + (2 * g + h) * q, q), q)]

    def own1(g, d, h):
        return send(fresh.at[2 * g + h], rows(me, g, h),
                    g1s.at[g, d, h], g1v.at[g, d, h], place(g, 0, step[d]))

    def own2(g, d, h):
        return send(fresh.at[2 * g + h], rows(me, g, h),
                    g2s.at[g, d, 0, h], g2v.at[g, d, 0, h], place(g, step[d], 0))

    def pass1(g, d):
        block = rows(place(g, 0, step[1 - d]), g, d)
        return send(block, block, f1s.at[g, d], f1v.at[g, d], place(g, 0, step[d]))

    away = (0, 1, 3, 2)

    def line2(g, d, e, h):
        block = rows(place(g, 0, away[e]), g, h)
        return send(block, block, g2s.at[g, d, e, h], g2v.at[g, d, e, h], place(g, step[d], 0))

    def pass2(g, d, e):
        block = rows(place(g, step[1 - d], away[e]), g, d)
        return send(block, block, f2s.at[g, d, e], f2v.at[g, d, e], place(g, step[d], 0))

    keep = []
    get_weight.wait()
    for h in range(2):
        for g in range(2):
            i = 2 * g + h
            for j in range(lanes):
                at = slice(128 * j, 128 * (j + 1))
                fresh[i, :, at] = (
                    wbuf[i * q:(i + 1) * q, at].astype(F32) - norm[i, :, at] * factor[j:j + 1]
                ).astype(BF16)
            own1(g, 0, h).start()
            own1(g, 1, h).start()
            own2(g, 0, h).start()
            own2(g, 1, h).start()
            keep.append(pltpu.make_async_copy(fresh.at[i], rows(me, g, h), o_sem.at[i]))
            keep[-1].start()
    for h in range(2):
        for g in range(2):
            for d in range(2):
                own1(g, 1 - d, h).wait_recv()
                if h == 1 - d:
                    pass1(g, 1 - d).start()
                line2(g, 0, 1 + d, h).start()
                line2(g, 1, 1 + d, h).start()
    for e in (0, 1, 2, 3):
        if e == 3:
            for g in range(2):
                for h in range(2):
                    pass1(g, h).wait_recv()
                    line2(g, 0, 3, h).start()
                    line2(g, 1, 3, h).start()
        for g in range(2):
            for d in range(2):
                if e == 0:
                    own2(g, d, d).wait_recv()
                else:
                    line2(g, d, e, d).wait_recv()
                pass2(g, d, e).start()

    for e in range(4):
        for g in range(2):
            for d in range(2):
                (own2(g, d, 1 - d) if e == 0 else line2(g, d, e, 1 - d)).wait_recv()
                pass2(g, d, e).wait_recv()
    for copy in keep:
        copy.wait()
    for g in range(2):
        for d in range(2):
            for m in range(SIDE):
                far1(g, d, m).wait_send()
                near1(g, d, m).wait_send()
                both1(g, d, m).wait_send()
            far2(g, d).wait_send()
            near2(g, d).wait_send()
            both2(g, d).wait_send()
            pass1(g, d).wait_send()
            for h in range(2):
                own1(g, d, h).wait_send()
                own2(g, d, h).wait_send()
                for e in range(1, 4):
                    line2(g, d, e, h).wait_send()
            for e in range(4):
                pass2(g, d, e).wait_send()
    for j in range(1, n):
        tell(j).wait_send()


def local(activations, cotangent, weight, row_state, column_state):
    tokens, width = activations.shape
    shard, ff = weight.shape
    q = shard // 4
    lanes = ff // 128
    dma = pltpu.SemaphoreType.DMA
    anywhere = pl.BlockSpec(memory_space=pl.ANY)
    vmem = pl.BlockSpec(memory_space=pltpu.VMEM)
    new_weight, row_moment, column_moment = pl.pallas_call(
        kernel,
        out_shape=(
            jax.ShapeDtypeStruct((width, ff), BF16),
            jax.ShapeDtypeStruct((4, q), F32),
            jax.ShapeDtypeStruct((lanes, 128), F32),
        ),
        in_specs=[anywhere, anywhere, anywhere, vmem, vmem],
        out_specs=(anywhere, vmem, vmem),
        scratch_shapes=[
            pltpu.VMEM((SLOTS, 2, tokens, 2 * q), BF16),
            pltpu.VMEM((tokens, ff), BF16),
            pltpu.VMEM((shard, ff), BF16),
            pltpu.VMEM((2, 4, 4, 2, q, ff), BF16),
            pltpu.VMEM((3, 2, 2, 4, q, ff), BF16),
            pltpu.VMEM((3, 2, 2, q, ff), BF16),
            pltpu.VMEM((4, q, ff), F32),
            pltpu.VMEM((4, q, ff), BF16),
            pltpu.VMEM((16, 128), F32),
            pltpu.VMEM((16, 16, 128), F32),
            dma((SLOTS, 2)), dma, dma, dma((4,)),
            dma((3, 2, 2, 4)), dma((3, 2, 2, 4)),
            dma((3, 2, 2)), dma((3, 2, 2)),
            dma((16,)), dma((16,)),
            dma((2, 2, 2)), dma((2, 2, 2)),
            dma((2, 2)), dma((2, 2)),
            dma((2, 2, 4, 2)), dma((2, 2, 4, 2)),
            dma((2, 2, 4)), dma((2, 2, 4)),
        ],
        compiler_params=pltpu.CompilerParams(
            collective_id=0, has_side_effects=True, vmem_limit_bytes=40 * 1024 * 1024
        ),
        cost_estimate=pl.CostEstimate(
            flops=2 * tokens * width * ff,
            bytes_accessed=2 * (tokens * (width + ff) + width * ff),
            transcendentals=shard,
        ),
    )(
        activations, cotangent, weight,
        row_state.reshape(4, q), column_state.reshape(lanes, 128),
    )
    return new_weight, row_moment.reshape(shard), column_moment.reshape(ff)


def solution(mesh):
    in_specs = (
        P(("section", "dp"), None),
        P(("section", "dp"), None),
        P(("section", "dp"), None),
        P(("section", "dp")),
        P("section"),
    )
    out_specs = (P("section", None), P(("section", "dp")), P("section"))
    return jax.shard_map(local, mesh=mesh, in_specs=in_specs, out_specs=out_specs, check_vma=False)
```

```python
import functools

import jax
import jax.numpy as jnp
from jax import lax
from jax.experimental import pallas as pl
from jax.experimental.pallas import tpu as pltpu
from jax.sharding import PartitionSpec as P

MESH = pl.DeviceIdType.MESH
decay_rate = 0.8
learn_rate = 0.1
clip_level = 1.0
epsilon_one = 1e-30
SIDE = 4
FAR, NEXT, LAST, OWN = 0, 1, 2, 3
SLOTS = 3
SHIFT = 12
PACE = 8
PIECES = 4
F32 = jnp.float32
BF16 = jnp.bfloat16


def offset(k):
    return 2 - k + (k // 2) * (7 - 2 * k)


def kernel(
    act, cot, weight, row_in, col_in,
    out, row_out, col_out,
    row_state, col_state, abuf, cbuf, wbuf, grad, r1, r2, norm, fresh, msg, heard,
    go_sem, a_sem, c_sem, w_sem, i_sem, o_sem,
    s1, v1, s2, v2, ss, vs, g1s, g1v, f1s, f1v, g2s, g2v, f2s, f2v,
):
    me = lax.axis_index("dp")
    px, pz = me // SIDE, me % SIDE
    section = lax.axis_index("section")
    late = 1 - section % 2
    twin = section + 1 - 2 * (section % 2)
    n = SIDE * SIDE
    q, ff = grad.shape[4], grad.shape[5]
    shard = 4 * q
    lanes = ff // 128

    def place(g, da, db):
        dx, dz = (da, db) if g == 0 else (db, da)
        return ((px + dx) % SIDE) * SIDE + (pz + dz) % SIDE

    def send(src, dst, ssem, rsem, target):
        return pltpu.make_async_remote_copy(
            src_ref=src, dst_ref=dst, send_sem=ssem, recv_sem=rsem,
            device_id={"dp": target}, device_id_type=MESH,
        )

    step = (1, SIDE - 1)

    def turn(i):
        i = (i + late * SHIFT) % (SIDE * SIDE)
        part = i // SIDE
        near = ((part + 1) // 2) % 2
        k = near * (NEXT + i % 2) + (part // OWN) * OWN
        return k, near * ((i - SIDE) // 2) + (1 - near) * (i % SIDE)

    def fetch(i, g):
        k, m = turn(i)
        col = place(g, offset(k), offset(m)) * shard + g * 2 * q
        return pltpu.make_async_copy(
            act.at[:, pl.ds(pl.multiple_of(col, 2 * q), 2 * q)],
            abuf.at[i % SLOTS, :, pl.ds(g * 2 * q, 2 * q)], a_sem.at[i % SLOTS, g],
        )

    barrier = pltpu.get_barrier_semaphore()
    for dx, dz in ((1, 0), (SIDE - 1, 0), (0, 1), (0, SIDE - 1)):
        pl.semaphore_signal(
            barrier, inc=1, device_id={"dp": place(0, dx, dz)}, device_id_type=MESH
        )
    pl.semaphore_signal(barrier, inc=1, device_id={"section": twin}, device_id_type=MESH)
    get_cot = pltpu.make_async_copy(cot, cbuf, c_sem)
    get_cot.start()
    for g in range(2):
        fetch(0, g).start()
    get_cot.wait()
    for i in range(1, SLOTS - 1):
        for g in range(2):
            fetch(i, g).start()
    get_weight = pltpu.make_async_copy(weight, wbuf, w_sem)
    get_weight.start()
    get_rows = pltpu.make_async_copy(row_in, row_state, i_sem.at[0])
    get_rows.start()
    get_cols = pltpu.make_async_copy(col_in, col_state, i_sem.at[1])
    get_cols.start()

    def far1(g, d, m):
        return send(grad.at[g, FAR, m, d], r1.at[0, g, d, m],
                    s1.at[0, g, d, m], v1.at[0, g, d, m], place(g, step[d], 0))

    def near1(g, d, m):
        return send(grad.at[g, NEXT + d, m, 1 - d], r1.at[1, g, d, m],
                    s1.at[1, g, d, m], v1.at[1, g, d, m], place(g, step[d], 0))

    def both1(g, d, m):
        return send(grad.at[g, NEXT + d, m, d], r1.at[2, g, d, m],
                    s1.at[2, g, d, m], v1.at[2, g, d, m], place(g, step[d], 0))

    @pl.loop(0, SIDE * SIDE)
    def _(i):
        k, m = turn(i)
        for g in range(2):
            fetch(i, g).wait()

        @pl.when(i + SLOTS - 1 < SIDE * SIDE)
        def _():
            for g in range(2):
                fetch(i + SLOTS - 1, g).start()

        part = lax.dot_general(
            abuf[i % SLOTS], cbuf[...], (((0,), (0,)), ((), ())),
            preferred_element_type=F32,
        ).astype(BF16)
        for g in range(2):
            for h in range(2):
                grad[g, k, m, h] = part[(2 * g + h) * q:(2 * g + h + 1) * q]

        @pl.when(i == 0)
        def _():
            pl.semaphore_wait(barrier, 5)

        @pl.when((1 - late) * i == PACE)
        def _():
            pl.semaphore_signal(go_sem, inc=1, device_id={"section": twin}, device_id_type=MESH)

        @pl.when(late * i == SIDE * SIDE - SHIFT)
        def _():
            pl.semaphore_wait(go_sem, 1)

        @pl.when(k == FAR)
        def _():
            for g in range(2):
                for d in range(2):
                    far1(g, d, m).start()

        for d in range(2):
            @pl.when(k == NEXT + d)
            def _():
                for g in range(2):
                    near1(g, d, m).start()

        for d in range(2):
            @pl.when(k == NEXT + d)
            def _():
                for g in range(2):
                    far1(g, d, m).wait_recv()
                    grad[g, NEXT + d, m, d] = (
                        grad[g, NEXT + d, m, d].astype(F32) + r1[0, g, d, m].astype(F32)
                    ).astype(BF16)
                    both1(g, d, m).start()

    def total1(g, m, h):
        both1(g, h, m).wait_recv()
        near1(g, 1 - h, m).wait_recv()
        return (
            grad[g, OWN, m, h].astype(F32) + r1[2, g, h, m].astype(F32)
        ) + r1[1, g, 1 - h, m].astype(F32)

    def far2(g, d):
        return send(grad.at[g, OWN, FAR, d], r2.at[0, g, d],
                    s2.at[0, g, d], v2.at[0, g, d], place(g, 0, step[d]))

    def near2(g, d):
        return send(grad.at[g, OWN, NEXT + d, 1 - d], r2.at[1, g, d],
                    s2.at[1, g, d], v2.at[1, g, d], place(g, 0, step[d]))

    def both2(g, d):
        return send(grad.at[g, OWN, NEXT + d, d], r2.at[2, g, d],
                    s2.at[2, g, d], v2.at[2, g, d], place(g, 0, step[d]))

    for g in range(2):
        for h in range(2):
            grad[g, OWN, FAR, h] = total1(g, FAR, h).astype(BF16)
            far2(g, h).start()
    for d in range(2):
        for g in range(2):
            for h in range(2):
                grad[g, OWN, NEXT + d, h] = total1(g, NEXT + d, h).astype(BF16)
            near2(g, d).start()
    for d in range(2):
        for g in range(2):
            far2(g, d).wait_recv()
            grad[g, OWN, NEXT + d, d] = (
                grad[g, OWN, NEXT + d, d].astype(F32) + r2[0, g, d].astype(F32)
            ).astype(BF16)
            both2(g, d).start()

    get_rows.wait()
    get_cols.wait()
    get_weight.wait()

    eye = lax.broadcasted_iota(jnp.int32, (q, q), 0) == lax.broadcasted_iota(jnp.int32, (q, q), 1)
    square_sum = jnp.zeros((1, ff), F32)
    update_sum = jnp.zeros((1, ff), F32)
    row_sum = jnp.zeros((1, 1), F32)
    for g in range(2):
        for h in range(2):
            i = 2 * g + h
            mine = total1(g, OWN, h)
            both2(g, h).wait_recv()
            near2(g, 1 - h).wait_recv()
            mine = (mine + r2[2, g, h].astype(F32)) + r2[1, g, 1 - h].astype(F32)
            squares = mine * mine + epsilon_one
            state = jnp.sum(jnp.where(eye, row_state[i:i + 1, :], 0.0), axis=1, keepdims=True)
            moment = decay_rate * state + (1.0 - decay_rate) * (
                jnp.sum(squares, axis=1, keepdims=True) / ff
            )
            row_out[i:i + 1, :] = jnp.sum(jnp.where(eye, moment, 0.0), axis=0, keepdims=True)
            scaled = mine * lax.rsqrt(moment)
            norm[i] = scaled
            square_sum += jnp.sum(squares, axis=0, keepdims=True)
            update_sum += jnp.sum(scaled * scaled, axis=0, keepdims=True)
            row_sum += jnp.sum(moment, axis=0, keepdims=True)
    msg[...] = jnp.zeros(msg.shape, F32)
    for j in range(lanes):
        msg[j:j + 1, :] = square_sum[:, 128 * j:128 * (j + 1)]
        msg[lanes + j:lanes + j + 1, :] = update_sum[:, 128 * j:128 * (j + 1)]
    msg[2 * lanes:2 * lanes + 1, :] = jnp.broadcast_to(row_sum, (1, 128))

    def tell(j):
        return send(msg, heard.at[me], ss.at[j], vs.at[me], (me + j) % n)

    def hear(j):
        other = (me + j) % n
        return send(msg, heard.at[other], ss.at[0], vs.at[other], other)

    for j in range(1, n):
        tell(j).start()
    heard[me] = msg[...]
    for j in range(1, n):
        hear(j).wait_recv()
    total = heard[0]
    for j in range(1, n):
        total = total + heard[j]
    col_moment = decay_rate * col_state[...] + (1.0 - decay_rate) * (total[:lanes] / (n * shard))
    col_out[...] = col_moment
    mean_row = jnp.max(total[2 * lanes:2 * lanes + 1], axis=1, keepdims=True) / (n * shard)
    update_mean = (
        jnp.sum(jnp.sum(total[lanes:2 * lanes] / col_moment, axis=1, keepdims=True), axis=0, keepdims=True)
        * mean_row / (n * shard * ff)
    )
    ratio = jnp.sqrt(update_mean) / clip_level
    factor = lax.rsqrt(col_moment) * (learn_rate * jnp.sqrt(mean_row) / jnp.maximum(1.0, ratio))

    def rows(dev, g, h):
        return out.at[pl.ds(pl.multiple_of(dev * shard + (2 * g + h) * q, q), q)]

    def own1(g, d, h):
        return send(fresh.at[2 * g + h], rows(me, g, h),
                    g1s.at[g, d, h], g1v.at[g, d, h], place(g, 0, step[d]))

    def own2(g, d, h):
        return send(fresh.at[2 * g + h], rows(me, g, h),
                    g2s.at[g, d, 0, h], g2v.at[g, d, 0, h], place(g, step[d], 0))

    def pass1(g, d):
        block = rows(place(g, 0, step[1 - d]), g, d)
        return send(block, block, f1s.at[g, d], f1v.at[g, d], place(g, 0, step[d]))

    away = (0, 1, 3, 2)

    def line2(g, d, e, h):
        block = rows(place(g, 0, away[e]), g, h)
        return send(block, block, g2s.at[g, d, e, h], g2v.at[g, d, e, h], place(g, step[d], 0))

    def pass2(g, d, e):
        block = rows(place(g, step[1 - d], away[e]), g, d)
        return send(block, block, f2s.at[g, d, e], f2v.at[g, d, e], place(g, step[d], 0))

    keep = []
    for h in range(2):
        for g in range(2):
            i = 2 * g + h
            for j in range(lanes):
                at = slice(128 * j, 128 * (j + 1))
                fresh[i, :, at] = (
                    wbuf[i * q:(i + 1) * q, at].astype(F32) - norm[i, :, at] * factor[j:j + 1]
                ).astype(BF16)
            own1(g, 0, h).start()
            own1(g, 1, h).start()
            own2(g, 0, h).start()
            own2(g, 1, h).start()
            keep.append(pltpu.make_async_copy(fresh.at[i], rows(me, g, h), o_sem.at[i]))
            keep[-1].start()
    for own in (True, False):
        for d in range(2):
            h = d if own else 1 - d
            for g in range(2):
                own1(g, d, h).wait_recv()
                if own:
                    pass1(g, d).start()
                line2(g, 0, 2 - d, h).start()
                line2(g, 1, 2 - d, h).start()
    for g in range(2):
        for h in range(2):
            pass1(g, h).wait_recv()
            line2(g, h, 3, h).start()
    for g in range(2):
        for h in range(2):
            line2(g, 1 - h, 3, h).start()
    for e in range(4):
        for g in range(2):
            for d in range(2):
                (own2(g, d, d) if e == 0 else line2(g, d, e, d)).wait_recv()
                pass2(g, d, e).start()

    for e in range(4):
        for g in range(2):
            for d in range(2):
                (own2(g, d, 1 - d) if e == 0 else line2(g, d, e, 1 - d)).wait_recv()
                pass2(g, d, e).wait_recv()
    for copy in keep:
        copy.wait()
    for g in range(2):
        for d in range(2):
            for m in range(SIDE):
                far1(g, d, m).wait_send()
                near1(g, d, m).wait_send()
                both1(g, d, m).wait_send()
            far2(g, d).wait_send()
            near2(g, d).wait_send()
            both2(g, d).wait_send()
            pass1(g, d).wait_send()
            for h in range(2):
                own1(g, d, h).wait_send()
                own2(g, d, h).wait_send()
                for e in range(1, 4):
                    line2(g, d, e, h).wait_send()
            for e in range(4):
                pass2(g, d, e).wait_send()
    for j in range(1, n):
        tell(j).wait_send()


def store(new, row, col, new_out, row_out, col_out, sem):
    span = new.shape[0] // PIECES
    copies = [
        pltpu.make_async_copy(
            new.at[pl.ds(i * span, span)], new_out.at[pl.ds(i * span, span)], sem.at[i]
        )
        for i in range(PIECES)
    ]
    copies.append(pltpu.make_async_copy(row, row_out, sem.at[PIECES]))
    copies.append(pltpu.make_async_copy(col, col_out, sem.at[PIECES + 1]))
    for copy in copies:
        copy.start()
    for copy in copies:
        copy.wait()


def local(activations, cotangent, weight, row_state, column_state):
    tokens, width = activations.shape
    shard, ff = weight.shape
    q = shard // 4
    lanes = ff // 128
    dma = pltpu.SemaphoreType.DMA
    anywhere = pl.BlockSpec(memory_space=pl.ANY)
    hbm = pl.BlockSpec(memory_space=pltpu.HBM)
    vmem = pl.BlockSpec(memory_space=pltpu.VMEM)
    new_weight, row_moment, column_moment = pl.pallas_call(
        kernel,
        out_shape=(
            pltpu.VMEM((width, ff), BF16),
            jax.ShapeDtypeStruct((4, q), F32),
            jax.ShapeDtypeStruct((lanes, 128), F32),
        ),
        in_specs=[hbm] * 5,
        out_specs=(vmem, vmem, vmem),
        scratch_shapes=[
            pltpu.VMEM((4, q), F32),
            pltpu.VMEM((lanes, 128), F32),
            pltpu.VMEM((SLOTS, tokens, 4 * q), BF16),
            pltpu.VMEM((tokens, ff), BF16),
            pltpu.VMEM((shard, ff), BF16),
            pltpu.VMEM((2, 4, 4, 2, q, ff), BF16),
            pltpu.VMEM((3, 2, 2, 4, q, ff), BF16),
            pltpu.VMEM((3, 2, 2, q, ff), BF16),
            pltpu.VMEM((4, q, ff), F32),
            pltpu.VMEM((4, q, ff), BF16),
            pltpu.VMEM((16, 128), F32),
            pltpu.VMEM((16, 16, 128), F32),
            pltpu.SemaphoreType.REGULAR,
            dma((SLOTS, 2)), dma, dma, dma((2,)), dma((4,)),
            dma((3, 2, 2, 4)), dma((3, 2, 2, 4)),
            dma((3, 2, 2)), dma((3, 2, 2)),
            dma((16,)), dma((16,)),
            dma((2, 2, 2)), dma((2, 2, 2)),
            dma((2, 2)), dma((2, 2)),
            dma((2, 2, 4, 2)), dma((2, 2, 4, 2)),
            dma((2, 2, 4)), dma((2, 2, 4)),
        ],
        compiler_params=pltpu.CompilerParams(
            collective_id=0, has_side_effects=True, vmem_limit_bytes=40 * 1024 * 1024
        ),
        cost_estimate=pl.CostEstimate(
            flops=2 * tokens * width * ff,
            bytes_accessed=2 * (tokens * (width + ff) + width * ff),
            transcendentals=shard,
        ),
    )(*(
        pltpu.with_memory_space_constraint(array, pltpu.HBM)
        for array in (
            activations, cotangent, weight,
            row_state.reshape(4, q), column_state.reshape(lanes, 128),
        )
    ))
    new_weight, row_moment, column_moment = pl.pallas_call(
        store,
        out_shape=(
            jax.ShapeDtypeStruct((width, ff), BF16),
            jax.ShapeDtypeStruct((4, q), F32),
            jax.ShapeDtypeStruct((lanes, 128), F32),
        ),
        in_specs=[vmem] * 3,
        out_specs=(hbm, hbm, hbm),
        scratch_shapes=[dma((PIECES + 2,))],
        compiler_params=pltpu.CompilerParams(vmem_limit_bytes=4 * 1024 * 1024),
    )(*(
        pltpu.with_memory_space_constraint(array, pltpu.VMEM)
        for array in (new_weight, row_moment, column_moment)
    ))
    return new_weight, row_moment.reshape(shard), column_moment.reshape(ff)


def solution(mesh):
    in_specs = (
        P(("section", "dp"), None),
        P(("section", "dp"), None),
        P(("section", "dp"), None),
        P(("section", "dp")),
        P("section"),
    )
    out_specs = (P("section", None), P(("section", "dp")), P("section"))
    return jax.shard_map(local, mesh=mesh, in_specs=in_specs, out_specs=out_specs, check_vma=False)
```

```python
import functools

import jax
import jax.numpy as jnp
from jax import lax
from jax.experimental import pallas as pl
from jax.experimental.pallas import tpu as pltpu
from jax.sharding import PartitionSpec as P

MESH = pl.DeviceIdType.MESH
decay_rate = 0.8
learn_rate = 0.1
clip_level = 1.0
epsilon_one = 1e-30
SIDE = 4
FAR, NEXT, LAST, OWN = 0, 1, 2, 3
SLOTS = 3
SHIFT = 12
PACE = 8
PIECES = 4
F32 = jnp.float32
BF16 = jnp.bfloat16


def offset(k):
    return 2 - k + (k // 2) * (7 - 2 * k)


def kernel(
    act, cot, weight, row_in, col_in,
    out, row_out, col_out,
    row_state, col_state, abuf, cbuf, wbuf, grad, r1, r2, norm, fresh, msg, heard,
    go_sem, first_sem, a_sem, w_sem, i_sem, o_sem,
    s1, v1, s2, v2, ss, vs, g1s, g1v, f1s, f1v, g2s, g2v, f2s, f2v, last_v,
):
    me = lax.axis_index("dp")
    px, pz = me // SIDE, me % SIDE
    section = lax.axis_index("section")
    late = 1 - section % 2
    twin = section + 1 - 2 * (section % 2)
    n = SIDE * SIDE
    q, ff = grad.shape[4], grad.shape[5]
    shard = 4 * q
    lanes = ff // 128

    def place(g, da, db):
        dx, dz = (da, db) if g == 0 else (db, da)
        return ((px + dx) % SIDE) * SIDE + (pz + dz) % SIDE

    def send(src, dst, ssem, rsem, target):
        return pltpu.make_async_remote_copy(
            src_ref=src, dst_ref=dst, send_sem=ssem, recv_sem=rsem,
            device_id={"dp": target}, device_id_type=MESH,
        )

    step = (1, SIDE - 1)

    def wait_for(like, sem):
        pltpu.make_async_copy(like, like, sem).wait()

    def turn(i):
        i = (i + late * SHIFT) % (SIDE * SIDE)
        part = i // SIDE
        near = ((part + 1) // 2) % 2
        k = near * (NEXT + i % 2) + (part // OWN) * OWN
        return k, near * ((i - SIDE) // 2) + (1 - near) * (i % SIDE)

    def fetch_refs(i, g):
        k, m = turn(i)
        col = place(g, offset(k), offset(m)) * shard + g * 2 * q
        return (
            act.at[:, pl.ds(pl.multiple_of(col, 2 * q), 2 * q)],
            abuf.at[i % SLOTS, :, pl.ds(g * 2 * q, 2 * q)],
        )

    def fetch(i, g):
        return pltpu.make_async_copy(*fetch_refs(i, g), a_sem.at[i % SLOTS])

    barrier = pltpu.get_barrier_semaphore()
    for dx, dz in ((1, 0), (SIDE - 1, 0), (0, 1), (0, SIDE - 1)):
        pl.semaphore_signal(
            barrier, inc=1, device_id={"dp": place(0, dx, dz)}, device_id_type=MESH
        )
    pl.semaphore_signal(barrier, inc=1, device_id={"section": twin}, device_id_type=MESH)
    get_cot = pltpu.make_async_copy(cot, cbuf, first_sem)
    get_cot.start()
    for i in range(SLOTS - 1):
        for g in range(2):
            fetch(i, g).start()
    get_weight = pltpu.make_async_copy(weight, wbuf, w_sem)
    get_weight.start()
    get_rows = pltpu.make_async_copy(row_in, row_state, i_sem.at[0])
    get_rows.start()
    get_cols = pltpu.make_async_copy(col_in, col_state, i_sem.at[1])
    get_cols.start()

    def far1(g, d, m):
        return send(grad.at[g, FAR, m, d], r1.at[0, g, d, m],
                    s1, v1.at[0, g, d, m], place(g, step[d], 0))

    def near1(g, d, m):
        return send(grad.at[g, NEXT + d, m, 1 - d], r1.at[1, g, d, m],
                    s1, v1.at[1, g, 1 - d, m], place(g, step[d], 0))

    def both1(g, d, m):
        return send(grad.at[g, NEXT + d, m, d], r1.at[2, g, d, m],
                    s1, v1.at[1, g, d, m], place(g, step[d], 0))

    @pl.loop(0, SIDE * SIDE)
    def _(i):
        k, m = turn(i)
        @pl.when(i + SLOTS - 1 < SIDE * SIDE)
        def _():
            for g in range(2):
                fetch(i + SLOTS - 1, g).start()

        @pl.when(i == 0)
        def _():
            get_cot.wait()

        wait_for(abuf.at[0], a_sem.at[i % SLOTS])
        part = lax.dot_general(
            abuf[i % SLOTS], cbuf[...], (((0,), (0,)), ((), ())),
            preferred_element_type=F32,
        ).astype(BF16)
        for g in range(2):
            for h in range(2):
                grad[g, k, m, h] = part[(2 * g + h) * q:(2 * g + h + 1) * q]

        @pl.when(i == 0)
        def _():
            pl.semaphore_wait(barrier, 5)

        @pl.when((1 - late) * i == PACE)
        def _():
            pl.semaphore_signal(go_sem, inc=1, device_id={"section": twin}, device_id_type=MESH)

        @pl.when(late * i == SIDE * SIDE - SHIFT)
        def _():
            pl.semaphore_wait(go_sem, 1)

        @pl.when(k == FAR)
        def _():
            for g in range(2):
                for d in range(2):
                    far1(g, d, m).start()

        for d in range(2):
            @pl.when(k == NEXT + d)
            def _():
                for g in range(2):
                    near1(g, d, m).start()

        for d in range(2):
            @pl.when(k == NEXT + d)
            def _():
                for g in range(2):
                    far1(g, d, m).wait_recv()
                    grad[g, NEXT + d, m, d] = (
                        grad[g, NEXT + d, m, d].astype(F32) + r1[0, g, d, m].astype(F32)
                    ).astype(BF16)
                    both1(g, d, m).start()

    def total1(g, m, h):
        wait_for(grad.at[g, OWN, m], v1.at[1, g, h, m])
        return (
            grad[g, OWN, m, h].astype(F32) + r1[2, g, h, m].astype(F32)
        ) + r1[1, g, 1 - h, m].astype(F32)

    def far2(g, d):
        return send(grad.at[g, OWN, FAR, d], r2.at[0, g, d],
                    s2, v2.at[0, g, d], place(g, 0, step[d]))

    def near2(g, d):
        return send(grad.at[g, OWN, NEXT + d, 1 - d], r2.at[1, g, d],
                    s2, v2.at[1, g, 1 - d], place(g, 0, step[d]))

    def both2(g, d):
        return send(grad.at[g, OWN, NEXT + d, d], r2.at[2, g, d],
                    s2, v2.at[1, g, d], place(g, 0, step[d]))

    for g in range(2):
        for h in range(2):
            grad[g, OWN, FAR, h] = total1(g, FAR, h).astype(BF16)
            far2(g, h).start()
    for d in range(2):
        for g in range(2):
            for h in range(2):
                grad[g, OWN, NEXT + d, h] = total1(g, NEXT + d, h).astype(BF16)
            near2(g, d).start()
    for d in range(2):
        for g in range(2):
            far2(g, d).wait_recv()
            grad[g, OWN, NEXT + d, d] = (
                grad[g, OWN, NEXT + d, d].astype(F32) + r2[0, g, d].astype(F32)
            ).astype(BF16)
            both2(g, d).start()

    get_rows.wait()
    get_cols.wait()
    get_weight.wait()

    eye = lax.broadcasted_iota(jnp.int32, (q, q), 0) == lax.broadcasted_iota(jnp.int32, (q, q), 1)
    square_sum = jnp.zeros((1, ff), F32)
    update_sum = jnp.zeros((1, ff), F32)
    row_sum = jnp.zeros((1, 1), F32)
    for g in range(2):
        for h in range(2):
            i = 2 * g + h
            mine = total1(g, OWN, h)
            wait_for(grad.at[g, OWN, OWN], v2.at[1, g, h])
            mine = (mine + r2[2, g, h].astype(F32)) + r2[1, g, 1 - h].astype(F32)
            squares = mine * mine + epsilon_one
            state = jnp.sum(jnp.where(eye, row_state[i:i + 1, :], 0.0), axis=1, keepdims=True)
            moment = decay_rate * state + (1.0 - decay_rate) * (
                jnp.sum(squares, axis=1, keepdims=True) / ff
            )
            row_out[i:i + 1, :] = jnp.sum(jnp.where(eye, moment, 0.0), axis=0, keepdims=True)
            scaled = mine * lax.rsqrt(moment)
            norm[i] = scaled
            square_sum += jnp.sum(squares, axis=0, keepdims=True)
            update_sum += jnp.sum(scaled * scaled, axis=0, keepdims=True)
            row_sum += jnp.sum(moment, axis=0, keepdims=True)
    msg[...] = jnp.zeros(msg.shape, F32)
    for j in range(lanes):
        msg[j:j + 1, :] = square_sum[:, 128 * j:128 * (j + 1)]
        msg[lanes + j:lanes + j + 1, :] = update_sum[:, 128 * j:128 * (j + 1)]
    msg[2 * lanes:2 * lanes + 1, :] = jnp.broadcast_to(row_sum, (1, 128))

    def tell(j):
        return send(msg, heard.at[me], ss, vs, (me + j) % n)

    for j in range(1, n):
        tell(j).start()
    heard[me] = msg[...]
    wait_for(heard.at[pl.ds(0, n - 1)], vs)
    total = heard[0]
    for j in range(1, n):
        total = total + heard[j]
    col_moment = decay_rate * col_state[...] + (1.0 - decay_rate) * (total[:lanes] / (n * shard))
    col_out[...] = col_moment
    mean_row = jnp.max(total[2 * lanes:2 * lanes + 1], axis=1, keepdims=True) / (n * shard)
    update_mean = (
        jnp.sum(jnp.sum(total[lanes:2 * lanes] / col_moment, axis=1, keepdims=True), axis=0, keepdims=True)
        * mean_row / (n * shard * ff)
    )
    ratio = jnp.sqrt(update_mean) / clip_level
    factor = lax.rsqrt(col_moment) * (learn_rate * jnp.sqrt(mean_row) / jnp.maximum(1.0, ratio))

    def rows(dev, g, h):
        return out.at[pl.ds(pl.multiple_of(dev * shard + (2 * g + h) * q, q), q)]

    def own1(g, d, h):
        return send(fresh.at[2 * g + h], rows(me, g, h),
                    g1s, g1v.at[g, d, h], place(g, 0, step[d]))

    def own2(g, d, h):
        return send(fresh.at[2 * g + h], rows(me, g, h),
                    g2s, g2v.at[g, d, 0] if h == d else last_v, place(g, step[d], 0))

    def pass1(g, d):
        block = rows(place(g, 0, step[1 - d]), g, d)
        return send(block, block, f1s, f1v.at[g, d], place(g, 0, step[d]))

    away = (0, 1, 3, 2)

    def line2(g, d, e, h):
        block = rows(place(g, 0, away[e]), g, h)
        return send(block, block, g2s, g2v.at[g, d, e] if h == d else last_v, place(g, step[d], 0))

    def pass2(g, d, e):
        block = rows(place(g, step[1 - d], away[e]), g, d)
        return send(block, block, f2s, f2v, place(g, step[d], 0))

    for h in range(2):
        for g in range(2):
            i = 2 * g + h
            for j in range(lanes):
                at = slice(128 * j, 128 * (j + 1))
                fresh[i, :, at] = (
                    wbuf[i * q:(i + 1) * q, at].astype(F32) - norm[i, :, at] * factor[j:j + 1]
                ).astype(BF16)
            own1(g, 0, h).start()
            own1(g, 1, h).start()
            own2(g, 0, h).start()
            own2(g, 1, h).start()
            pltpu.make_async_copy(fresh.at[i], rows(me, g, h), o_sem).start()
    wait_for(r1, s1)
    wait_for(r2, s2)
    wait_for(heard.at[pl.ds(0, n - 1)], ss)
    for own in (True, False):
        for d in range(2):
            h = d if own else 1 - d
            for g in range(2):
                own1(g, d, h).wait_recv()
                if own:
                    pass1(g, d).start()
                line2(g, 0, 2 - d, h).start()
                line2(g, 1, 2 - d, h).start()
    for g in range(2):
        for h in range(2):
            pass1(g, h).wait_recv()
            line2(g, h, 3, h).start()
    for g in range(2):
        for h in range(2):
            line2(g, 1 - h, 3, h).start()
    for e in range(4):
        for g in range(2):
            for d in range(2):
                (own2(g, d, d) if e == 0 else line2(g, d, e, d)).wait_recv()
                pass2(g, d, e).start()

    wait_for(fresh, o_sem)
    wait_for(grad.at[0, 0], g1s)
    wait_for(r2.at[0], f1s)
    wait_for(grad.at[0], g2s)
    wait_for(grad.at[0, 0:2], last_v)
    wait_for(grad.at[0, 0:2], f2v)
    wait_for(grad.at[0, 0:2], f2s)


def store(new, row, col, new_out, row_out, col_out, sem):
    span = new.shape[0] // PIECES
    copies = [
        pltpu.make_async_copy(
            new.at[pl.ds(i * span, span)], new_out.at[pl.ds(i * span, span)], sem.at[i]
        )
        for i in range(PIECES)
    ]
    copies.append(pltpu.make_async_copy(row, row_out, sem.at[PIECES]))
    copies.append(pltpu.make_async_copy(col, col_out, sem.at[PIECES + 1]))
    for copy in copies:
        copy.start()
    for copy in copies:
        copy.wait()


def local(activations, cotangent, weight, row_state, column_state):
    tokens, width = activations.shape
    shard, ff = weight.shape
    q = shard // 4
    lanes = ff // 128
    dma = pltpu.SemaphoreType.DMA
    anywhere = pl.BlockSpec(memory_space=pl.ANY)
    hbm = pl.BlockSpec(memory_space=pltpu.HBM)
    vmem = pl.BlockSpec(memory_space=pltpu.VMEM)
    new_weight, row_moment, column_moment = pl.pallas_call(
        kernel,
        out_shape=(
            pltpu.VMEM((width, ff), BF16),
            jax.ShapeDtypeStruct((4, q), F32),
            jax.ShapeDtypeStruct((lanes, 128), F32),
        ),
        in_specs=[hbm] * 5,
        out_specs=(anywhere, vmem, vmem),
        scratch_shapes=[
            pltpu.VMEM((4, q), F32),
            pltpu.VMEM((lanes, 128), F32),
            pltpu.VMEM((SLOTS, tokens, 4 * q), BF16),
            pltpu.VMEM((tokens, ff), BF16),
            pltpu.VMEM((shard, ff), BF16),
            pltpu.VMEM((2, 4, 4, 2, q, ff), BF16),
            pltpu.VMEM((3, 2, 2, 4, q, ff), BF16),
            pltpu.VMEM((3, 2, 2, q, ff), BF16),
            pltpu.VMEM((4, q, ff), F32),
            pltpu.VMEM((4, q, ff), BF16),
            pltpu.VMEM((16, 128), F32),
            pltpu.VMEM((16, 16, 128), F32),
            pltpu.SemaphoreType.REGULAR,
            dma, dma((SLOTS,)), dma, dma((2,)), dma,
            dma, dma((2, 2, 2, 4)), dma, dma((2, 2, 2)), dma, dma,
            dma, dma((2, 2, 2)), dma, dma((2, 2)),
            dma, dma((2, 2, 4)), dma, dma, dma,
        ],
        compiler_params=pltpu.CompilerParams(
            collective_id=0, has_side_effects=True, vmem_limit_bytes=40 * 1024 * 1024
        ),
        cost_estimate=pl.CostEstimate(
            flops=2 * tokens * width * ff,
            bytes_accessed=2 * (tokens * (width + ff) + width * ff),
            transcendentals=shard,
        ),
    )(*(
        pltpu.with_memory_space_constraint(array, pltpu.HBM)
        for array in (
            activations, cotangent, weight,
            row_state.reshape(4, q), column_state.reshape(lanes, 128),
        )
    ))
    new_weight, row_moment, column_moment = pl.pallas_call(
        store,
        out_shape=(
            jax.ShapeDtypeStruct((width, ff), BF16),
            jax.ShapeDtypeStruct((4, q), F32),
            jax.ShapeDtypeStruct((lanes, 128), F32),
        ),
        in_specs=[vmem] * 3,
        out_specs=(hbm, hbm, hbm),
        scratch_shapes=[dma((PIECES + 2,))],
        compiler_params=pltpu.CompilerParams(vmem_limit_bytes=4 * 1024 * 1024),
    )(*(
        pltpu.with_memory_space_constraint(array, pltpu.VMEM)
        for array in (new_weight, row_moment, column_moment)
    ))
    return new_weight, row_moment.reshape(shard), column_moment.reshape(ff)


def solution(mesh):
    in_specs = (
        P(("section", "dp"), None),
        P(("section", "dp"), None),
        P(("section", "dp"), None),
        P(("section", "dp")),
        P("section"),
    )
    out_specs = (P("section", None), P(("section", "dp")), P("section"))
    return jax.shard_map(local, mesh=mesh, in_specs=in_specs, out_specs=out_specs, check_vma=False)
```

```python
import functools

import jax
import jax.numpy as jnp
from jax import lax
from jax.experimental import pallas as pl
from jax.experimental.pallas import tpu as pltpu
from jax.sharding import PartitionSpec as P

MESH = pl.DeviceIdType.MESH
decay_rate = 0.8
learn_rate = 0.1
clip_level = 1.0
epsilon_one = 1e-30
SIDE = 4
FAR, NEXT, LAST, OWN = 0, 1, 2, 3
SLOTS = 3
SHIFT = 12
PACE = 8
PIECES = 4
F32 = jnp.float32
BF16 = jnp.bfloat16


def offset(k):
    return 2 - k + (k // 2) * (7 - 2 * k)


def kernel(
    act, cot, weight, row_in, col_in,
    out, row_out, col_out,
    row_state, col_state, abuf, cbuf, wbuf, grad, r1, r2, norm, fresh, msg, heard,
    go_sem, first_sem, a_sem, w_sem, i_sem, o_sem,
    s1, far_v, near_v, s2, v2, ss, vs, g1s, g1v, f1s, f1v, g2s, g2v, f2s, f2v, last_v,
):
    me = lax.axis_index("dp")
    px, pz = me // SIDE, me % SIDE
    section = lax.axis_index("section")
    late = 1 - section % 2
    twin = section + 1 - 2 * (section % 2)
    n = SIDE * SIDE
    q, ff = grad.shape[4], grad.shape[5]
    shard = 4 * q
    lanes = ff // 128

    def place(g, da, db):
        dx, dz = (da, db) if g == 0 else (db, da)
        return ((px + dx) % SIDE) * SIDE + (pz + dz) % SIDE

    def send(src, dst, ssem, rsem, target):
        return pltpu.make_async_remote_copy(
            src_ref=src, dst_ref=dst, send_sem=ssem, recv_sem=rsem,
            device_id={"dp": target}, device_id_type=MESH,
        )

    step = (1, SIDE - 1)

    def wait_for(like, sem):
        pltpu.make_async_copy(like, like, sem).wait()

    two, four = grad.at[0, 0, 0], grad.at[0, 0, 0:2]

    def turn(i):
        i = (i + late * SHIFT) % (SIDE * SIDE)
        part = i // SIDE
        near = ((part + 1) // 2) % 2
        k = near * (NEXT + i % 2) + (part // OWN) * OWN
        return k, near * ((i - SIDE) // 2) + (1 - near) * (i % SIDE)

    def fetch_refs(i, g):
        k, m = turn(i)
        col = place(g, offset(k), offset(m)) * shard + g * 2 * q
        return (
            act.at[:, pl.ds(pl.multiple_of(col, 2 * q), 2 * q)],
            abuf.at[i % SLOTS, :, pl.ds(g * 2 * q, 2 * q)],
        )

    def fetch(i, g):
        return pltpu.make_async_copy(*fetch_refs(i, g), a_sem.at[i % SLOTS])

    barrier = pltpu.get_barrier_semaphore()
    for dx, dz in ((1, 0), (SIDE - 1, 0), (0, 1), (0, SIDE - 1)):
        pl.semaphore_signal(
            barrier, inc=1, device_id={"dp": place(0, dx, dz)}, device_id_type=MESH
        )
    pl.semaphore_signal(barrier, inc=1, device_id={"section": twin}, device_id_type=MESH)
    get_cot = pltpu.make_async_copy(cot, cbuf, first_sem)
    get_cot.start()
    for i in range(SLOTS - 1):
        for g in range(2):
            fetch(i, g).start()
    get_weight = pltpu.make_async_copy(weight, wbuf, w_sem)
    get_weight.start()
    get_rows = pltpu.make_async_copy(row_in, row_state, i_sem.at[0])
    get_rows.start()
    get_cols = pltpu.make_async_copy(col_in, col_state, i_sem.at[1])
    get_cols.start()

    def far1(g, d, m):
        return send(grad.at[g, FAR, m, d], r1.at[0, g, d, m],
                    s1, far_v.at[d, m], place(g, step[d], 0))

    def near1(g, d, m):
        return send(grad.at[g, NEXT + d, m, 1 - d], r1.at[1, g, d, m],
                    s1, near_v.at[1 - d, m], place(g, step[d], 0))

    def both1(g, d, m):
        return send(grad.at[g, NEXT + d, m, d], r1.at[2, g, d, m],
                    s1, near_v.at[d, m], place(g, step[d], 0))

    @pl.loop(0, SIDE * SIDE)
    def _(i):
        k, m = turn(i)
        @pl.when(i + SLOTS - 1 < SIDE * SIDE)
        def _():
            for g in range(2):
                fetch(i + SLOTS - 1, g).start()

        @pl.when(i == 0)
        def _():
            get_cot.wait()

        wait_for(abuf.at[0], a_sem.at[i % SLOTS])
        part = lax.dot_general(
            abuf[i % SLOTS], cbuf[...], (((0,), (0,)), ((), ())),
            preferred_element_type=F32,
        ).astype(BF16)
        for g in range(2):
            for h in range(2):
                grad[g, k, m, h] = part[(2 * g + h) * q:(2 * g + h + 1) * q]

        @pl.when(i == 0)
        def _():
            pl.semaphore_wait(barrier, 5)

        @pl.when((1 - late) * i == PACE)
        def _():
            pl.semaphore_signal(go_sem, inc=1, device_id={"section": twin}, device_id_type=MESH)

        @pl.when(late * i == SIDE * SIDE - SHIFT)
        def _():
            pl.semaphore_wait(go_sem, 1)

        @pl.when(k == FAR)
        def _():
            for g in range(2):
                for d in range(2):
                    far1(g, d, m).start()

        for d in range(2):
            @pl.when(k == NEXT + d)
            def _():
                for g in range(2):
                    near1(g, d, m).start()

        for d in range(2):
            @pl.when(k == NEXT + d)
            def _():
                wait_for(two, far_v.at[d, m])
                for g in range(2):
                    grad[g, NEXT + d, m, d] = (
                        grad[g, NEXT + d, m, d].astype(F32) + r1[0, g, d, m].astype(F32)
                    ).astype(BF16)
                    both1(g, d, m).start()

    def ready1(m, h):
        wait_for(four, near_v.at[h, m])

    def total1(g, m, h):
        return (
            grad[g, OWN, m, h].astype(F32) + r1[2, g, h, m].astype(F32)
        ) + r1[1, g, 1 - h, m].astype(F32)

    def far2(g, d):
        return send(grad.at[g, OWN, FAR, d], r2.at[0, g, d],
                    s2, v2.at[0, d], place(g, 0, step[d]))

    def near2(g, d):
        return send(grad.at[g, OWN, NEXT + d, 1 - d], r2.at[1, g, d],
                    s2, v2.at[1, 1 - d], place(g, 0, step[d]))

    def both2(g, d):
        return send(grad.at[g, OWN, NEXT + d, d], r2.at[2, g, d],
                    s2, v2.at[1, d], place(g, 0, step[d]))

    for h in range(2):
        ready1(FAR, h)
        for g in range(2):
            grad[g, OWN, FAR, h] = total1(g, FAR, h).astype(BF16)
            far2(g, h).start()
    for d in range(2):
        for h in range(2):
            ready1(NEXT + d, h)
            for g in range(2):
                grad[g, OWN, NEXT + d, h] = total1(g, NEXT + d, h).astype(BF16)
        for g in range(2):
            near2(g, d).start()
    for d in range(2):
        wait_for(two, v2.at[0, d])
        for g in range(2):
            grad[g, OWN, NEXT + d, d] = (
                grad[g, OWN, NEXT + d, d].astype(F32) + r2[0, g, d].astype(F32)
            ).astype(BF16)
            both2(g, d).start()

    get_rows.wait()
    get_cols.wait()
    get_weight.wait()

    eye = lax.broadcasted_iota(jnp.int32, (q, q), 0) == lax.broadcasted_iota(jnp.int32, (q, q), 1)
    square_sum = jnp.zeros((1, ff), F32)
    update_sum = jnp.zeros((1, ff), F32)
    row_sum = jnp.zeros((1, 1), F32)
    for h in range(2):
        ready1(OWN, h)
        wait_for(four, v2.at[1, h])
        for g in range(2):
            i = 2 * g + h
            mine = total1(g, OWN, h)
            mine = (mine + r2[2, g, h].astype(F32)) + r2[1, g, 1 - h].astype(F32)
            squares = mine * mine + epsilon_one
            state = jnp.sum(jnp.where(eye, row_state[i:i + 1, :], 0.0), axis=1, keepdims=True)
            moment = decay_rate * state + (1.0 - decay_rate) * (
                jnp.sum(squares, axis=1, keepdims=True) / ff
            )
            row_out[i:i + 1, :] = jnp.sum(jnp.where(eye, moment, 0.0), axis=0, keepdims=True)
            scaled = mine * lax.rsqrt(moment)
            norm[i] = scaled
            square_sum += jnp.sum(squares, axis=0, keepdims=True)
            update_sum += jnp.sum(scaled * scaled, axis=0, keepdims=True)
            row_sum += jnp.sum(moment, axis=0, keepdims=True)
    msg[...] = jnp.zeros(msg.shape, F32)
    for j in range(lanes):
        msg[j:j + 1, :] = square_sum[:, 128 * j:128 * (j + 1)]
        msg[lanes + j:lanes + j + 1, :] = update_sum[:, 128 * j:128 * (j + 1)]
    msg[2 * lanes:2 * lanes + 1, :] = jnp.broadcast_to(row_sum, (1, 128))

    def tell(j):
        return send(msg, heard.at[me], ss, vs, (me + j) % n)

    for j in range(1, n):
        tell(j).start()
    heard[me] = msg[...]
    wait_for(heard.at[pl.ds(0, n - 1)], vs)
    total = heard[0]
    for j in range(1, n):
        total = total + heard[j]
    col_moment = decay_rate * col_state[...] + (1.0 - decay_rate) * (total[:lanes] / (n * shard))
    col_out[...] = col_moment
    mean_row = jnp.max(total[2 * lanes:2 * lanes + 1], axis=1, keepdims=True) / (n * shard)
    update_mean = (
        jnp.sum(jnp.sum(total[lanes:2 * lanes] / col_moment, axis=1, keepdims=True), axis=0, keepdims=True)
        * mean_row / (n * shard * ff)
    )
    ratio = jnp.sqrt(update_mean) / clip_level
    factor = lax.rsqrt(col_moment) * (learn_rate * jnp.sqrt(mean_row) / jnp.maximum(1.0, ratio))

    def rows(dev, g, h):
        return out.at[pl.ds(pl.multiple_of(dev * shard + (2 * g + h) * q, q), q)]

    def own1(g, d, h):
        return send(fresh.at[2 * g + h], rows(me, g, h),
                    g1s, g1v.at[d, h], place(g, 0, step[d]))

    def own2(g, d, h):
        return send(fresh.at[2 * g + h], rows(me, g, h),
                    g2s, g2v.at[d, 0] if h == d else last_v, place(g, step[d], 0))

    def pass1(g, d):
        block = rows(place(g, 0, step[1 - d]), g, d)
        return send(block, block, f1s, f1v.at[d], place(g, 0, step[d]))

    away = (0, 1, 3, 2)

    def line2(g, d, e, h):
        block = rows(place(g, 0, away[e]), g, h)
        return send(block, block, g2s, g2v.at[d, e] if h == d else last_v, place(g, step[d], 0))

    def pass2(g, d, e):
        block = rows(place(g, step[1 - d], away[e]), g, d)
        return send(block, block, f2s, f2v, place(g, step[d], 0))

    for h in range(2):
        for g in range(2):
            i = 2 * g + h
            for j in range(lanes):
                at = slice(128 * j, 128 * (j + 1))
                fresh[i, :, at] = (
                    wbuf[i * q:(i + 1) * q, at].astype(F32) - norm[i, :, at] * factor[j:j + 1]
                ).astype(BF16)
            own1(g, 0, h).start()
            own1(g, 1, h).start()
            own2(g, 0, h).start()
            own2(g, 1, h).start()
            pltpu.make_async_copy(fresh.at[i], rows(me, g, h), o_sem).start()
    wait_for(r1, s1)
    wait_for(r2, s2)
    wait_for(heard.at[pl.ds(0, n - 1)], ss)
    for own in (True, False):
        for d in range(2):
            h = d if own else 1 - d
            wait_for(two, g1v.at[d, h])
            for g in range(2):
                if own:
                    pass1(g, d).start()
                line2(g, 0, 2 - d, h).start()
                line2(g, 1, 2 - d, h).start()
    for h in range(2):
        wait_for(two, f1v.at[h])
        for g in range(2):
            line2(g, h, 3, h).start()
    for h in range(2):
        for g in range(2):
            line2(g, 1 - h, 3, h).start()
    for e in range(4):
        for d in range(2):
            wait_for(two, g2v.at[d, e])
            for g in range(2):
                pass2(g, d, e).start()

    wait_for(fresh, o_sem)
    wait_for(grad.at[0, 0], g1s)
    wait_for(r2.at[0], f1s)
    wait_for(grad.at[0], g2s)
    wait_for(grad.at[0, 0:2], last_v)
    wait_for(grad.at[0, 0:2], f2v)
    wait_for(grad.at[0, 0:2], f2s)


def store(new, row, col, new_out, row_out, col_out, sem):
    span = new.shape[0] // PIECES
    copies = [
        pltpu.make_async_copy(
            new.at[pl.ds(i * span, span)], new_out.at[pl.ds(i * span, span)], sem.at[i]
        )
        for i in range(PIECES)
    ]
    copies.append(pltpu.make_async_copy(row, row_out, sem.at[PIECES]))
    copies.append(pltpu.make_async_copy(col, col_out, sem.at[PIECES + 1]))
    for copy in copies:
        copy.start()
    for copy in copies:
        copy.wait()


def local(activations, cotangent, weight, row_state, column_state):
    tokens, width = activations.shape
    shard, ff = weight.shape
    q = shard // 4
    lanes = ff // 128
    dma = pltpu.SemaphoreType.DMA
    anywhere = pl.BlockSpec(memory_space=pl.ANY)
    hbm = pl.BlockSpec(memory_space=pltpu.HBM)
    vmem = pl.BlockSpec(memory_space=pltpu.VMEM)
    new_weight, row_moment, column_moment = pl.pallas_call(
        kernel,
        out_shape=(
            pltpu.VMEM((width, ff), BF16),
            jax.ShapeDtypeStruct((4, q), F32),
            jax.ShapeDtypeStruct((lanes, 128), F32),
        ),
        in_specs=[hbm] * 5,
        out_specs=(anywhere, vmem, vmem),
        scratch_shapes=[
            pltpu.VMEM((4, q), F32),
            pltpu.VMEM((lanes, 128), F32),
            pltpu.VMEM((SLOTS, tokens, 4 * q), BF16),
            pltpu.VMEM((tokens, ff), BF16),
            pltpu.VMEM((shard, ff), BF16),
            pltpu.VMEM((2, 4, 4, 2, q, ff), BF16),
            pltpu.VMEM((3, 2, 2, 4, q, ff), BF16),
            pltpu.VMEM((3, 2, 2, q, ff), BF16),
            pltpu.VMEM((4, q, ff), F32),
            pltpu.VMEM((4, q, ff), BF16),
            pltpu.VMEM((16, 128), F32),
            pltpu.VMEM((16, 16, 128), F32),
            pltpu.SemaphoreType.REGULAR,
            dma, dma((SLOTS,)), dma, dma((2,)), dma,
            dma, dma((2, 4)), dma((2, 4)), dma, dma((2, 2)), dma, dma,
            dma, dma((2, 2)), dma, dma((2,)),
            dma, dma((2, 4)), dma, dma, dma,
        ],
        compiler_params=pltpu.CompilerParams(
            collective_id=0, has_side_effects=True, vmem_limit_bytes=40 * 1024 * 1024
        ),
        cost_estimate=pl.CostEstimate(
            flops=2 * tokens * width * ff,
            bytes_accessed=2 * (tokens * (width + ff) + width * ff),
            transcendentals=shard,
        ),
    )(*(
        pltpu.with_memory_space_constraint(array, pltpu.HBM)
        for array in (
            activations, cotangent, weight,
            row_state.reshape(4, q), column_state.reshape(lanes, 128),
        )
    ))
    new_weight, row_moment, column_moment = pl.pallas_call(
        store,
        out_shape=(
            jax.ShapeDtypeStruct((width, ff), BF16),
            jax.ShapeDtypeStruct((4, q), F32),
            jax.ShapeDtypeStruct((lanes, 128), F32),
        ),
        in_specs=[vmem] * 3,
        out_specs=(hbm, hbm, hbm),
        scratch_shapes=[dma((PIECES + 2,))],
        compiler_params=pltpu.CompilerParams(vmem_limit_bytes=4 * 1024 * 1024),
    )(*(
        pltpu.with_memory_space_constraint(array, pltpu.VMEM)
        for array in (new_weight, row_moment, column_moment)
    ))
    return new_weight, row_moment.reshape(shard), column_moment.reshape(ff)


def solution(mesh):
    in_specs = (
        P(("section", "dp"), None),
        P(("section", "dp"), None),
        P(("section", "dp"), None),
        P(("section", "dp")),
        P("section"),
    )
    out_specs = (P("section", None), P(("section", "dp")), P("section"))
    return jax.shard_map(local, mesh=mesh, in_specs=in_specs, out_specs=out_specs, check_vma=False)
```

```python
import functools

import jax
import jax.numpy as jnp
from jax import lax
from jax.experimental import pallas as pl
from jax.experimental.pallas import tpu as pltpu
from jax.sharding import PartitionSpec as P

MESH = pl.DeviceIdType.MESH
decay_rate = 0.8
learn_rate = 0.1
clip_level = 1.0
epsilon_one = 1e-30
SIDE = 4
FAR, NEXT, LAST, OWN = 0, 1, 2, 3
SLOTS = 3
SHIFT = 12
PACE = 8
PIECES = 4
F32 = jnp.float32
BF16 = jnp.bfloat16


def offset(k):
    return 2 - k + (k // 2) * (7 - 2 * k)


def kernel(
    act, cot, weight, row_in, col_in,
    out, row_out, col_out,
    row_state, col_state, abuf, cbuf, wbuf, grad, r1, r2, norm, fresh, msg, heard,
    go_sem, first_sem, a_sem, w_sem, i_sem, o_sem,
    s1, far_v, near_v, s2, v2, ss, vs, g1s, g1v, f1s, f1v, g2s, g2v, f2s, f2v, last_v,
):
    me = lax.axis_index("dp")
    px, pz = me // SIDE, me % SIDE
    section = lax.axis_index("section")
    late = 1 - section % 2
    twin = section + 1 - 2 * (section % 2)
    n = SIDE * SIDE
    q, ff = grad.shape[4], grad.shape[5]
    shard = 4 * q
    lanes = ff // 128

    def place(g, da, db):
        dx, dz = (da, db) if g == 0 else (db, da)
        return ((px + dx) % SIDE) * SIDE + (pz + dz) % SIDE

    def send(src, dst, ssem, rsem, target):
        return pltpu.make_async_remote_copy(
            src_ref=src, dst_ref=dst, send_sem=ssem, recv_sem=rsem,
            device_id={"dp": target}, device_id_type=MESH,
        )

    step = (1, SIDE - 1)

    def wait_for(like, sem):
        pltpu.make_async_copy(like, like, sem).wait()

    two, four = grad.at[0, 0, 0], grad.at[0, 0, 0:2]

    def turn(i):
        i = (i + late * SHIFT) % (SIDE * SIDE)
        part = i // SIDE
        near = ((part + 1) // 2) % 2
        k = near * (NEXT + i % 2) + (part // OWN) * OWN
        return k, near * ((i - SIDE) // 2) + (1 - near) * (i % SIDE)

    def chunk(k, g, c):
        near = ((k + 1) // 2) % 2
        return near * (NEXT + c) + (1 - near) * k, c + near * (LAST - k) * (1 - 2 * c)

    def fetch(i, g, c):
        k, m = turn(i)
        kc, h = chunk(k, g, c)
        col = place(g, offset(kc), offset(m)) * shard + (2 * g + h) * q
        return pltpu.make_async_copy(
            act.at[:, pl.ds(pl.multiple_of(col, q), q)],
            abuf.at[i % SLOTS, :, pl.ds((2 * g + c) * q, q)],
            a_sem.at[i % SLOTS],
        )

    barrier = pltpu.get_barrier_semaphore()
    for dx, dz in ((1, 0), (SIDE - 1, 0), (0, 1), (0, SIDE - 1)):
        pl.semaphore_signal(
            barrier, inc=1, device_id={"dp": place(0, dx, dz)}, device_id_type=MESH
        )
    pl.semaphore_signal(barrier, inc=1, device_id={"section": twin}, device_id_type=MESH)
    get_cot = pltpu.make_async_copy(cot, cbuf, first_sem)
    get_cot.start()
    for i in range(SLOTS - 1):
        for g in range(2):
            for c in range(2):
                fetch(i, g, c).start()
    get_weight = pltpu.make_async_copy(weight, wbuf, w_sem)
    get_weight.start()
    get_rows = pltpu.make_async_copy(row_in, row_state, i_sem.at[0])
    get_rows.start()
    get_cols = pltpu.make_async_copy(col_in, col_state, i_sem.at[1])
    get_cols.start()

    def far1(g, d, m):
        return send(grad.at[g, FAR, m, d], r1.at[0, g, d, m],
                    s1, far_v.at[d, m], place(g, step[d], 0))

    def near1(g, d, m):
        return send(grad.at[g, NEXT + d, m, 1 - d], r1.at[1, g, d, m],
                    s1, near_v.at[1 - d, m], place(g, step[d], 0))

    def both1(g, d, m):
        return send(grad.at[g, NEXT + d, m, d], r1.at[2, g, d, m],
                    s1, near_v.at[d, m], place(g, step[d], 0))

    @pl.loop(0, SIDE * SIDE)
    def _(i):
        k, m = turn(i)
        @pl.when(i + SLOTS - 1 < SIDE * SIDE)
        def _():
            for g in range(2):
                for c in range(2):
                    fetch(i + SLOTS - 1, g, c).start()

        @pl.when(i == 0)
        def _():
            get_cot.wait()

        wait_for(abuf.at[0], a_sem.at[i % SLOTS])
        part = lax.dot_general(
            abuf[i % SLOTS], cbuf[...], (((0,), (0,)), ((), ())),
            preferred_element_type=F32,
        ).astype(BF16)
        for g in range(2):
            for c in range(2):
                kc, h = chunk(k, g, c)
                grad[g, kc, m, h] = part[(2 * g + c) * q:(2 * g + c + 1) * q]

        @pl.when(i == 0)
        def _():
            pl.semaphore_wait(barrier, 5)

        @pl.when((1 - late) * i == PACE)
        def _():
            pl.semaphore_signal(go_sem, inc=1, device_id={"section": twin}, device_id_type=MESH)

        @pl.when(late * i == SIDE * SIDE - SHIFT)
        def _():
            pl.semaphore_wait(go_sem, 1)

        @pl.when(k == FAR)
        def _():
            for g in range(2):
                for d in range(2):
                    far1(g, d, m).start()

        @pl.when(k == NEXT)
        def _():
            for g in range(2):
                for d in range(2):
                    near1(g, d, m).start()

        @pl.when(k == LAST)
        def _():
            for d in range(2):
                wait_for(two, far_v.at[d, m])
                for g in range(2):
                    grad[g, NEXT + d, m, d] = (
                        grad[g, NEXT + d, m, d].astype(F32) + r1[0, g, d, m].astype(F32)
                    ).astype(BF16)
                    both1(g, d, m).start()

    def ready1(m, h):
        wait_for(four, near_v.at[h, m])

    def total1(g, m, h):
        return (
            grad[g, OWN, m, h].astype(F32) + r1[2, g, h, m].astype(F32)
        ) + r1[1, g, 1 - h, m].astype(F32)

    def far2(g, d):
        return send(grad.at[g, OWN, FAR, d], r2.at[0, g, d],
                    s2, v2.at[0, d], place(g, 0, step[d]))

    def near2(g, d):
        return send(grad.at[g, OWN, NEXT + d, 1 - d], r2.at[1, g, d],
                    s2, v2.at[1, 1 - d], place(g, 0, step[d]))

    def both2(g, d):
        return send(grad.at[g, OWN, NEXT + d, d], r2.at[2, g, d],
                    s2, v2.at[1, d], place(g, 0, step[d]))

    for h in range(2):
        ready1(FAR, h)
        for g in range(2):
            grad[g, OWN, FAR, h] = total1(g, FAR, h).astype(BF16)
            far2(g, h).start()
    for d in range(2):
        for h in range(2):
            ready1(NEXT + d, h)
            for g in range(2):
                grad[g, OWN, NEXT + d, h] = total1(g, NEXT + d, h).astype(BF16)
        for g in range(2):
            near2(g, d).start()
    for d in range(2):
        wait_for(two, v2.at[0, d])
        for g in range(2):
            grad[g, OWN, NEXT + d, d] = (
                grad[g, OWN, NEXT + d, d].astype(F32) + r2[0, g, d].astype(F32)
            ).astype(BF16)
            both2(g, d).start()

    get_rows.wait()
    get_cols.wait()
    get_weight.wait()

    eye = lax.broadcasted_iota(jnp.int32, (q, q), 0) == lax.broadcasted_iota(jnp.int32, (q, q), 1)
    square_sum = jnp.zeros((1, ff), F32)
    update_sum = jnp.zeros((1, ff), F32)
    row_sum = jnp.zeros((1, 1), F32)
    for h in range(2):
        ready1(OWN, h)
        wait_for(four, v2.at[1, h])
        for g in range(2):
            i = 2 * g + h
            mine = total1(g, OWN, h)
            mine = (mine + r2[2, g, h].astype(F32)) + r2[1, g, 1 - h].astype(F32)
            squares = mine * mine + epsilon_one
            state = jnp.sum(jnp.where(eye, row_state[i:i + 1, :], 0.0), axis=1, keepdims=True)
            moment = decay_rate * state + (1.0 - decay_rate) * (
                jnp.sum(squares, axis=1, keepdims=True) / ff
            )
            row_out[i:i + 1, :] = jnp.sum(jnp.where(eye, moment, 0.0), axis=0, keepdims=True)
            scaled = mine * lax.rsqrt(moment)
            norm[i] = scaled
            square_sum += jnp.sum(squares, axis=0, keepdims=True)
            update_sum += jnp.sum(scaled * scaled, axis=0, keepdims=True)
            row_sum += jnp.sum(moment, axis=0, keepdims=True)
    msg[...] = jnp.zeros(msg.shape, F32)
    for j in range(lanes):
        msg[j:j + 1, :] = square_sum[:, 128 * j:128 * (j + 1)]
        msg[lanes + j:lanes + j + 1, :] = update_sum[:, 128 * j:128 * (j + 1)]
    msg[2 * lanes:2 * lanes + 1, :] = jnp.broadcast_to(row_sum, (1, 128))

    def tell(j):
        return send(msg, heard.at[me], ss, vs, (me + j) % n)

    for j in range(1, n):
        tell(j).start()
    heard[me] = msg[...]
    wait_for(heard.at[pl.ds(0, n - 1)], vs)
    total = heard[0]
    for j in range(1, n):
        total = total + heard[j]
    col_moment = decay_rate * col_state[...] + (1.0 - decay_rate) * (total[:lanes] / (n * shard))
    col_out[...] = col_moment
    mean_row = jnp.max(total[2 * lanes:2 * lanes + 1], axis=1, keepdims=True) / (n * shard)
    update_mean = (
        jnp.sum(jnp.sum(total[lanes:2 * lanes] / col_moment, axis=1, keepdims=True), axis=0, keepdims=True)
        * mean_row / (n * shard * ff)
    )
    ratio = jnp.sqrt(update_mean) / clip_level
    factor = lax.rsqrt(col_moment) * (learn_rate * jnp.sqrt(mean_row) / jnp.maximum(1.0, ratio))

    def rows(dev, g, h):
        return out.at[pl.ds(pl.multiple_of(dev * shard + (2 * g + h) * q, q), q)]

    def own1(g, d, h):
        return send(fresh.at[2 * g + h], rows(me, g, h),
                    g1s, g1v.at[d, h], place(g, 0, step[d]))

    def own2(g, d, h):
        return send(fresh.at[2 * g + h], rows(me, g, h),
                    g2s, g2v.at[d, 0] if h == d else last_v, place(g, step[d], 0))

    def pass1(g, d):
        block = rows(place(g, 0, step[1 - d]), g, d)
        return send(block, block, f1s, f1v.at[d], place(g, 0, step[d]))

    away = (0, 1, 3, 2)

    def line2(g, d, e, h):
        block = rows(place(g, 0, away[e]), g, h)
        return send(block, block, g2s, g2v.at[d, e] if h == d else last_v, place(g, step[d], 0))

    def pass2(g, d, e):
        block = rows(place(g, step[1 - d], away[e]), g, d)
        return send(block, block, f2s, f2v, place(g, step[d], 0))

    for h in range(2):
        for g in range(2):
            i = 2 * g + h
            for j in range(lanes):
                at = slice(128 * j, 128 * (j + 1))
                fresh[i, :, at] = (
                    wbuf[i * q:(i + 1) * q, at].astype(F32) - norm[i, :, at] * factor[j:j + 1]
                ).astype(BF16)
            own1(g, 0, h).start()
            own1(g, 1, h).start()
            own2(g, 0, h).start()
            own2(g, 1, h).start()
            pltpu.make_async_copy(fresh.at[i], rows(me, g, h), o_sem).start()
    wait_for(r1, s1)
    wait_for(r2, s2)
    wait_for(heard.at[pl.ds(0, n - 1)], ss)
    for own in (True, False):
        for d in range(2):
            h = d if own else 1 - d
            wait_for(two, g1v.at[d, h])
            for g in range(2):
                if own:
                    pass1(g, d).start()
                line2(g, 0, 2 - d, h).start()
                line2(g, 1, 2 - d, h).start()
    for h in range(2):
        wait_for(two, f1v.at[h])
        for g in range(2):
            line2(g, h, 3, h).start()
    for h in range(2):
        for g in range(2):
            line2(g, 1 - h, 3, h).start()
    for e in range(4):
        for d in range(2):
            wait_for(two, g2v.at[d, e])
            for g in range(2):
                pass2(g, d, e).start()

    wait_for(fresh, o_sem)
    wait_for(grad.at[0, 0], g1s)
    wait_for(r2.at[0], f1s)
    wait_for(grad.at[0], g2s)
    wait_for(grad.at[0, 0:2], last_v)
    wait_for(grad.at[0, 0:2], f2v)
    wait_for(grad.at[0, 0:2], f2s)


def store(new, row, col, new_out, row_out, col_out, sem):
    span = new.shape[0] // PIECES
    copies = [
        pltpu.make_async_copy(
            new.at[pl.ds(i * span, span)], new_out.at[pl.ds(i * span, span)], sem.at[i]
        )
        for i in range(PIECES)
    ]
    copies.append(pltpu.make_async_copy(row, row_out, sem.at[PIECES]))
    copies.append(pltpu.make_async_copy(col, col_out, sem.at[PIECES + 1]))
    for copy in copies:
        copy.start()
    for copy in copies:
        copy.wait()


def local(activations, cotangent, weight, row_state, column_state):
    tokens, width = activations.shape
    shard, ff = weight.shape
    q = shard // 4
    lanes = ff // 128
    dma = pltpu.SemaphoreType.DMA
    anywhere = pl.BlockSpec(memory_space=pl.ANY)
    hbm = pl.BlockSpec(memory_space=pltpu.HBM)
    vmem = pl.BlockSpec(memory_space=pltpu.VMEM)
    new_weight, row_moment, column_moment = pl.pallas_call(
        kernel,
        out_shape=(
            pltpu.VMEM((width, ff), BF16),
            jax.ShapeDtypeStruct((4, q), F32),
            jax.ShapeDtypeStruct((lanes, 128), F32),
        ),
        in_specs=[hbm] * 5,
        out_specs=(anywhere, vmem, vmem),
        scratch_shapes=[
            pltpu.VMEM((4, q), F32),
            pltpu.VMEM((lanes, 128), F32),
            pltpu.VMEM((SLOTS, tokens, 4 * q), BF16),
            pltpu.VMEM((tokens, ff), BF16),
            pltpu.VMEM((shard, ff), BF16),
            pltpu.VMEM((2, 4, 4, 2, q, ff), BF16),
            pltpu.VMEM((3, 2, 2, 4, q, ff), BF16),
            pltpu.VMEM((3, 2, 2, q, ff), BF16),
            pltpu.VMEM((4, q, ff), F32),
            pltpu.VMEM((4, q, ff), BF16),
            pltpu.VMEM((16, 128), F32),
            pltpu.VMEM((16, 16, 128), F32),
            pltpu.SemaphoreType.REGULAR,
            dma, dma((SLOTS,)), dma, dma((2,)), dma,
            dma, dma((2, 4)), dma((2, 4)), dma, dma((2, 2)), dma, dma,
            dma, dma((2, 2)), dma, dma((2,)),
            dma, dma((2, 4)), dma, dma, dma,
        ],
        compiler_params=pltpu.CompilerParams(
            collective_id=0, has_side_effects=True, vmem_limit_bytes=40 * 1024 * 1024
        ),
        cost_estimate=pl.CostEstimate(
            flops=2 * tokens * width * ff,
            bytes_accessed=2 * (tokens * (width + ff) + width * ff),
            transcendentals=shard,
        ),
    )(*(
        pltpu.with_memory_space_constraint(array, pltpu.HBM)
        for array in (
            activations, cotangent, weight,
            row_state.reshape(4, q), column_state.reshape(lanes, 128),
        )
    ))
    new_weight, row_moment, column_moment = pl.pallas_call(
        store,
        out_shape=(
            jax.ShapeDtypeStruct((width, ff), BF16),
            jax.ShapeDtypeStruct((4, q), F32),
            jax.ShapeDtypeStruct((lanes, 128), F32),
        ),
        in_specs=[vmem] * 3,
        out_specs=(hbm, hbm, hbm),
        scratch_shapes=[dma((PIECES + 2,))],
        compiler_params=pltpu.CompilerParams(vmem_limit_bytes=4 * 1024 * 1024),
    )(*(
        pltpu.with_memory_space_constraint(array, pltpu.VMEM)
        for array in (new_weight, row_moment, column_moment)
    ))
    return new_weight, row_moment.reshape(shard), column_moment.reshape(ff)


def solution(mesh):
    in_specs = (
        P(("section", "dp"), None),
        P(("section", "dp"), None),
        P(("section", "dp"), None),
        P(("section", "dp")),
        P("section"),
    )
    out_specs = (P("section", None), P(("section", "dp")), P("section"))
    return jax.shard_map(local, mesh=mesh, in_specs=in_specs, out_specs=out_specs, check_vma=False)
```
